256 devices in a mesh: ind: 8 (over x, core), var: 32 (over z, y).
Axes of the slice: x: 4, y: 4, z: 8, core: 2. Of those that a mesh axis runs over, the one named last changes fastest.
Arguments:
- dosages: bfloat16 [131072, 8192], P('ind', 'var'), may hold values from -4 to 4
- phenotypes: float32 [32, 131072], P(None, 'ind'), may hold values from -6 to 6
- screen_ids: int32 [32, 256], P('var'), may hold values from 0 to 255, each once within a row
- screen_counts: int32 [32], P('var'), may hold values from 1 to 192, 2048 in all
- kkt_ids: int32 [32, 64], P('var'), may hold values from 0 to 255
- coef_prev: float32 [32, 6144], P(None, 'var'), may hold values from -3 to 3
- coef_slope: float32 [32, 6144], P(None, 'var'), may hold values from -3 to 3
- penalty: float32 [32], replicated, may hold values from 0.02 to 0.4
Outputs:
- coefficients: float32 [32, 6144], P(None, 'var')
- residual: float32 [32, 131072], P(None, ('ind', 'var'))
- kkt_grad: float32 [32, 2048], P(None, 'var')
- max_violation: float32 [32], replicated
- objective: float32 [32], replicated
The draws below stay inside these ranges and needn't reach their ends.
Inputs may be any that keep to these rules, and one draw needn't show every extreme that they name: `screen_ids`: each row names every one of the owner's 256 candidate columns once. `screen_counts`: the counts sum to 2048; some owner has exactly 192 live slots.
All inputs are finite; a program needn't handle non-finite values. No bound on the sum of `screen_counts` on one device may be relied on, other than what follows from the above.
Results may differ from the reference program's by a relative error of at most 0.0051.
Values may be sent and summed in bfloat16 or wider, within the bound.
A program may use at most 128 MiB of HBM per device.

```python
import math
import jax
import jax.numpy as jnp
import numpy as np
from jax import lax

K = 32
POOL_DEV = 256
KKT_DEV = 64
SWEEPS = 2
CAP = 192
SLOTS = 6144
SCREEN = 2048
POOL = 8192
ROWS = 131072
N_VAR = 32


def place_ends(entries, rng, smallest, high):
    longest = entries.shape.index(max(entries.shape))
    spots = []
    for shift in (0, 1):
        where = [jax.random.randint(jax.random.fold_in(rng, axis), (), 0, length) for axis, length in enumerate(entries.shape)]
        where[longest] = (where[longest] + shift) % entries.shape[longest]
        spots.append(tuple(where))
    return entries.at[spots[0]].set(smallest).at[spots[1]].set(high)


def block_scale(stream_key, extent, shards, low, largest):
    def one(position, blocks):
        heights = jax.random.uniform(jax.random.fold_in(jax.random.fold_in(stream_key, 6), position), (blocks,), jnp.float32, low / len(shards), largest / len(shards))
        return jnp.repeat(jnp.exp(heights), extent[position] // blocks).reshape((-1,) + (1,) * (len(extent) - position - 1))

    factor_of = one(*shards[0])
    for cut in shards[1:]:
        factor_of = factor_of * one(*cut)
    return factor_of


def split_up(amount, total, most, lean):
    weights = [(1 << 20) // math.isqrt(grade ** lean) + 1 for grade in range(2, amount + 1)]
    spare, counts = total - most - (amount - 1), [1] * (amount - 1)
    while spare > 0:
        movable = [i for i in range(amount - 1) if counts[i] < most]
        pool, budget = sum([weights[i] for i in movable]), spare
        for i in movable:
            more = min(most - counts[i], max(1, budget * weights[i] // pool), spare)
            counts[i] = counts[i] + more
            spare = spare - more
    return np.array([most] + counts)


def uneven(rng, count, total, reach, lean):
    if count == 2:
        one = jax.random.randint(rng, (), max(1, total - reach), min(reach, total - 1) + 1)
        return jnp.stack([one, total - one])
    tallies = jnp.asarray(split_up(count, total, reach, lean), jnp.int32)
    couples = (count - 1) // 2
    donor, taker = tallies[1:1 + 2 * couples:2], tallies[2:2 + 2 * couples:2]
    margin = jnp.minimum(donor - 1, reach - taker)
    moved = jax.random.randint(jax.random.fold_in(rng, 1), (couples,), 0, 1 << 20) % (margin + 1)
    tallies = tallies.at[1:1 + 2 * couples:2].set(donor - moved).at[2:2 + 2 * couples:2].set(taker + moved)
    return tallies[jax.random.permutation(jax.random.fold_in(rng, 2), count)]


def bell_draw(rng, dims, deviation, reach, pieces=(), kind=jnp.bfloat16):
    level = block_scale(rng, dims, pieces, -0.22, 0.18) if pieces else 1.0
    entries = jax.random.normal(rng, dims, jnp.float32) * deviation * level
    return jnp.minimum(jnp.maximum(entries, -reach), reach).astype(kind)


def setup_inputs(seed: int = 0) -> dict:
    keys = jax.random.split(jax.random.key(seed), 9)
    return {
        "dosages": bell_draw(keys[0], (ROWS, POOL), 1.0, 4.0, ((0, 8), (1, 32))),
        "phenotypes": bell_draw(keys[1], (K, ROWS), 1.0, 6.0, ((1, 8),), jnp.float32),
        "screen_ids": jax.vmap(lambda own: jax.random.permutation(own, POOL_DEV))(jax.random.split(keys[2], N_VAR)).reshape((N_VAR, POOL_DEV)).astype(jnp.int32),
        "screen_counts": uneven(keys[3], N_VAR, SCREEN, CAP, 2).astype(jnp.int32),
        "kkt_ids": place_ends(jax.random.randint(keys[4], (N_VAR, KKT_DEV), 0, POOL_DEV), jax.random.fold_in(keys[4], 1), 0, POOL_DEV - 1).astype(jnp.int32),
        "coef_prev": bell_draw(keys[5], (K, SLOTS), 0.5, 3.0, ((1, 32),), jnp.float32),
        "coef_slope": bell_draw(keys[6], (K, SLOTS), 0.4, 3.0, ((1, 32),), jnp.float32),
        "penalty": jnp.clip(jnp.exp(jax.random.uniform(keys[7], (K,), jnp.float32, math.log(0.02), math.log(0.4))), 0.02, 0.4),
    }


def owner_block(dosages, owner):
    blocks = dosages.reshape(ROWS, N_VAR, POOL_DEV)
    return lax.dynamic_index_in_dim(blocks, owner, 1, keepdims=False)


def predict(dosages, screen_ids, coef):
    coef_bf = coef.astype(jnp.bfloat16).reshape(K, N_VAR, CAP)

    def step(total, owner):
        cols = jnp.take(owner_block(dosages, owner), screen_ids[owner, :CAP], axis=1)
        part = lax.dynamic_index_in_dim(coef_bf, owner, 1, keepdims=False)
        term = lax.dot_general(part, cols, (((1,), (1,)), ((), ())), preferred_element_type=jnp.float32)
        return total + term, 0

    owners = jnp.arange(N_VAR, dtype=jnp.int32)
    total, unused = lax.scan(step, jnp.zeros((K, ROWS), jnp.float32), owners)
    return total


def contract(dosages, ids, resid_bf):
    def one(owner):
        cols = jnp.take(owner_block(dosages, owner), ids[owner], axis=1)
        return lax.dot_general(resid_bf, cols, (((1,), (0,)), ((), ())), preferred_element_type=jnp.float32)

    owners = jnp.arange(N_VAR, dtype=jnp.int32)
    parts = lax.map(one, owners)
    return jnp.transpose(parts, (1, 0, 2)).reshape(K, -1) / ROWS


def reference(dosages, phenotypes, screen_ids, screen_counts, kkt_ids, coef_prev, coef_slope, penalty):
    slot = jnp.arange(CAP, dtype=jnp.int32)[None, :]
    live = (slot < screen_counts[:, None]).astype(jnp.float32).reshape(1, SLOTS)
    screen_cap = screen_ids[:, :CAP]
    shrink = 0.25 * penalty[:, None]
    ridge = 1.0 + 0.25 * penalty[:, None]
    coef = live * (coef_prev + 0.5 * coef_slope)
    for sweep in range(SWEEPS):
        resid = phenotypes - predict(dosages, screen_ids, coef)
        grad = contract(dosages, screen_cap, resid.astype(jnp.bfloat16))
        moved = coef + 0.5 * grad
        coef = live * jnp.sign(moved) * jnp.maximum(jnp.abs(moved) - shrink, 0.0) / ridge
    resid = phenotypes - predict(dosages, screen_ids, coef)
    kkt_grad = contract(dosages, kkt_ids, resid.astype(jnp.bfloat16))
    max_violation = jnp.max(jnp.maximum(jnp.abs(kkt_grad) - 0.5 * penalty[:, None], 0.0), axis=1)
    loss = jnp.sum(resid * resid, axis=1) / (2.0 * ROWS)
    pen_sum = penalty * jnp.sum(0.5 * jnp.abs(coef) + 0.25 * coef * coef, axis=1)
    return coef, resid, kkt_grad, max_violation, loss + pen_sum
```

```python
import functools

import jax
import jax.numpy as jnp
from jax import lax
from jax.experimental import pallas as pl
from jax.experimental.pallas import tpu as pltpu
from jax.sharding import PartitionSpec as P

MESH = pl.DeviceIdType.MESH
SWEEPS = 2
ROUNDS = SWEEPS + 1
NY, NZ = 4, 8
NIND = 8
CHUNKS = 4
NT = (((1,), (1,)), ((), ()))
Y_ORDER = (2, 1, 3)
Z_ORDER = (4, 3, 5, 2, 6, 1, 7)
ORDER = sorted(
    ((phase, chunk) for phase in range(1, 6) for chunk in range(CHUNKS)),
    key=lambda step: (step[1] + (0, 0, 1.5, 3, 4.5, 6)[step[0]], -step[0]),
)


def dot(a, b, **options):
    return jnp.dot(a, b, preferred_element_type=jnp.float32, **options)


def kernel(
    total_rows,
    dosages, phenotypes, screen_ids, screen_counts, kkt_ids, coef_prev, coef_slope, penalty,
    coef_out, resid_out, kkt_out, small_out,
    x, phen, psend, yrecv, zsend, zown, zrecv, gathered, isend, irecv, fsend, frecv, fz, fzrecv,
    x_sem, phen_sem, y_s, y_r, z_s, z_r, gz_s, gz_r, gy_s, gy_r, i_s, i_r, f_s, f_r,
):
    ind = lax.axis_index("ind")
    var = lax.axis_index("var")
    z, y = var // NY, lax.rem(var, NY)
    k, cap = coef_prev.shape
    width = x.shape[3]
    pool = x.shape[4]
    share = CHUNKS * width

    def at_y(step):
        return lax.rem(y + step, NY)

    def at_z(step):
        return lax.rem(z + step, NZ)

    def y_peer(step):
        return (ind, z * NY + at_y(step))

    def z_peer(step):
        return (ind, at_z(step) * NY + y)

    def i_peer(step):
        return (lax.rem(ind + step, NIND), var)

    x_copies = [
        pltpu.make_async_copy(dosages.at[:, :, c], x.at[c], x_sem.at[c]) for c in range(CHUNKS)
    ]
    for copy in x_copies:
        copy.start()
    phen_copy = pltpu.make_async_copy(
        phenotypes.at[:, pl.ds(pl.multiple_of(var * share, share), share)], phen, phen_sem
    )
    phen_copy.start()

    barrier = pltpu.get_barrier_semaphore()
    for step in range(1, NY):
        pl.semaphore_signal(barrier, inc=1, device_id=y_peer(step), device_id_type=MESH)
    for step in range(1, NZ):
        pl.semaphore_signal(barrier, inc=1, device_id=z_peer(step), device_id_type=MESH)
    for step in range(1, NIND):
        pl.semaphore_signal(barrier, inc=1, device_id=i_peer(step), device_id_type=MESH)

    live = (lax.broadcasted_iota(jnp.int32, (1, cap), 1) < screen_counts[0]).astype(jnp.float32)
    spread = (lax.broadcasted_iota(jnp.int32, (pool, cap), 0) == screen_ids[:, :cap]).astype(jnp.float32)
    batch = kkt_ids.shape[1]
    pick = (lax.broadcasted_iota(jnp.int32, (pool, batch), 0) == kkt_ids[...]).astype(jnp.float32)
    diagonal = lax.broadcasted_iota(jnp.int32, (k, k), 0) == lax.broadcasted_iota(jnp.int32, (k, k), 1)
    pen = jnp.sum(jnp.where(diagonal, jnp.broadcast_to(penalty[...], (k, k)), 0.0), axis=1, keepdims=True)
    shrink = 0.25 * pen
    ridge = 1.0 + 0.25 * pen
    exact = dict(preferred_element_type=jnp.float32, precision=lax.Precision.HIGHEST)
    warm = live * (coef_prev[...] + 0.5 * coef_slope[...])
    coef = lax.dot_general(warm, spread, NT, **exact)
    live_col = lax.dot_general(jnp.broadcast_to(live, (k, cap)), spread, NT, **exact)

    def remote(src, dst, send, recv, device):
        return pltpu.make_async_remote_copy(
            src_ref=src, dst_ref=dst, send_sem=send, recv_sem=recv, device_id=device, device_id_type=MESH
        )

    def drain(ref, sem):
        pltpu.make_async_copy(ref, ref, sem).wait()

    for r in range(ROUNDS):
        coef_bf = coef.astype(jnp.bfloat16)
        total = jnp.zeros((k, pool), jnp.float32)
        squares = jnp.zeros((k, 128), jnp.float32)
        for phase, c in ORDER:
            if phase == 1:
                if r == 0:
                    x_copies[c].wait()
                for step in Y_ORDER + (0,):
                    to = at_y(step)
                    for t in range(NZ):
                        psend[c, to, t] = lax.dot_general(
                            coef_bf, x[c, t, to], NT, preferred_element_type=jnp.float32
                        ).astype(jnp.bfloat16)
                    if r == 0 and c == 0 and step == Y_ORDER[0]:
                        pl.semaphore_wait(barrier, NY + NZ + NIND - 3)
                    if step:
                        remote(
                            psend.at[c, to], yrecv.at[r, c, step - 1], y_s.at[r, c], y_r.at[r, c], y_peer(step)
                        ).start()
            elif phase == 2:
                drain(yrecv.at[r, c], y_r.at[r, c])
                for step in Z_ORDER + (0,):
                    to = at_z(step)
                    part = psend[c, y, to].astype(jnp.float32)
                    for s in range(NY - 1):
                        part = part + yrecv[r, c, s, to].astype(jnp.float32)
                    if step:
                        zsend[c, to] = part.astype(jnp.bfloat16)
                        remote(
                            zsend.at[c, to], zrecv.at[r, c, step - 1], z_s.at[r, c], z_r.at[r, c], z_peer(step)
                        ).start()
                    else:
                        zown[c] = part
            elif phase == 3:
                drain(zrecv.at[r, c], z_r.at[r, c])
                if r == 0 and c == 0:
                    phen_copy.wait()
                pred = zown[c]
                for s in range(NZ - 1):
                    pred = pred + zrecv[r, c, s].astype(jnp.float32)
                columns = slice(c * width, (c + 1) * width)
                resid = phen[:, columns] - pred
                if r == ROUNDS - 1:
                    resid_out[:, columns] = resid
                gathered[r, c, y, z] = resid.astype(jnp.bfloat16)
                for step in Z_ORDER:
                    block = gathered.at[r, c, y, z]
                    remote(block, block, gz_s.at[r, c], gz_r.at[r, c], z_peer(step)).start()
            else:
                if phase == 4:
                    drain(gathered.at[r, c, y, pl.ds(0, NZ - 1)], gz_r.at[r, c])
                    for step in Y_ORDER:
                        blocks = gathered.at[r, c, y]
                        remote(blocks, blocks, gy_s.at[r, c], gy_r.at[r, c], y_peer(step)).start()
                else:
                    drain(gathered.at[r, c, pl.ds(0, NY - 1)], gy_r.at[r, c])
                for step in (0,) if phase == 4 else (1, 2, 3):
                    of = at_y(step)
                    for t in range(NZ):
                        block = gathered[r, c, of, t]
                        total = total + dot(block, x[c, t, of])
                        if r == ROUNDS - 1:
                            wide = block.astype(jnp.float32)
                            for lane in range(0, width, 128):
                                piece = wide[:, lane:lane + 128]
                                squares = squares + piece * piece
        last = r == ROUNDS - 1
        if last:
            loss = jnp.sum(squares, axis=1, keepdims=True)
            kkt_part = dot(total, pick, precision=lax.Precision.HIGHEST)
            total = jnp.concatenate([kkt_part, jnp.broadcast_to(loss, (k, 128 - batch))], axis=1)
            isend[r, :, :128] = total
            dst = irecv.at[r, :, :, pl.ds(0, 128)]
            src = isend.at[r, :, pl.ds(0, 128)]
        else:
            isend[r] = total
            dst = irecv.at[r]
            src = isend.at[r]
        for step in range(1, NIND):
            remote(src, dst.at[ind], i_s.at[r], i_r.at[r], i_peer(step)).start()
        if last:
            irecv[r, ind, :, :128] = total
        else:
            irecv[r, ind] = total
        for c in range(CHUNKS):
            drain(yrecv.at[r, c], y_s.at[r, c])
            drain(zrecv.at[r, c], z_s.at[r, c])
            drain(zrecv.at[r, c], gz_s.at[r, c])
            drain(yrecv.at[r, c], gy_s.at[r, c])
        others = dst.at[pl.ds(0, NIND - 1)]
        drain(others, i_r.at[r])
        total = irecv[r, 0, :, :128] if last else irecv[r, 0]
        for s in range(1, NIND):
            total = total + (irecv[r, s, :, :128] if last else irecv[r, s])
        drain(others, i_s.at[r])
        if not last:
            moved = coef + 0.5 * (total / total_rows)
            coef = live_col * (jnp.maximum(moved - shrink, 0.0) + jnp.minimum(moved + shrink, 0.0)) / ridge

    kkt_grad = total[:, :batch] / total_rows
    kkt_out[...] = kkt_grad
    loss = total[:, batch:batch + 1] / (2.0 * total_rows)
    worst = jnp.max(jnp.maximum(jnp.abs(kkt_grad) - 0.5 * pen, 0.0), axis=1, keepdims=True)
    pen_part = pen * jnp.sum(0.5 * jnp.abs(coef) + 0.25 * coef * coef, axis=1, keepdims=True)

    rows = lax.broadcasted_iota(jnp.int32, (k, 128), 0)
    lanes = lax.broadcasted_iota(jnp.int32, (k, 128), 1)

    def as_row(column):
        return jnp.sum(jnp.where(rows == lanes, column, 0.0), axis=0, keepdims=True)

    upper = lax.broadcasted_iota(jnp.int32, (8, 128), 0) == 0
    fsend[...] = jnp.where(upper, as_row(worst), as_row(pen_part))

    def merge(a, b):
        return jnp.where(upper, jnp.maximum(a, b), a + b)

    for step in Y_ORDER:
        remote(fsend, frecv.at[y], f_s.at[0], f_r.at[0], y_peer(step)).start()
    frecv[y] = fsend[...]
    coef_out[...] = dot(coef, spread, precision=lax.Precision.HIGHEST)
    drain(frecv.at[pl.ds(0, NY - 1)], f_r.at[0])
    both = frecv[0]
    for s in range(1, NY):
        both = merge(both, frecv[s])
    fz[...] = both
    for step in Z_ORDER:
        remote(fz, fzrecv.at[z], f_s.at[1], f_r.at[1], z_peer(step)).start()
    fzrecv[z] = both
    drain(fzrecv.at[pl.ds(0, NZ - 1)], f_r.at[1])
    both = fzrecv[0]
    for s in range(1, NZ):
        both = merge(both, fzrecv[s])
    small_out[...] = jnp.where(upper, both, both + as_row(loss))
    drain(frecv.at[pl.ds(0, NY - 1)], f_s.at[0])
    drain(fzrecv.at[pl.ds(0, NZ - 1)], f_s.at[1])


def body(dosages, phenotypes, screen_ids, screen_counts, kkt_ids, coef_prev, coef_slope, penalty):
    row_dev, pool = dosages.shape
    k, cap = coef_prev.shape
    batch = kkt_ids.shape[1]
    n_var = lax.axis_size("var")
    share = row_dev // n_var
    width = share // CHUNKS
    bf, f32 = jnp.bfloat16, jnp.float32
    vmem = pl.BlockSpec(memory_space=pltpu.VMEM)
    hbm = pl.BlockSpec(memory_space=pl.ANY)
    smem = pl.BlockSpec(memory_space=pltpu.SMEM)
    dma = pltpu.SemaphoreType.DMA
    coef, resid, kkt, small = pl.pallas_call(
        functools.partial(kernel, row_dev * lax.axis_size("ind")),
        out_shape=(
            jax.ShapeDtypeStruct((k, cap), f32),
            jax.ShapeDtypeStruct((k, share), f32),
            jax.ShapeDtypeStruct((k, batch), f32),
            jax.ShapeDtypeStruct((8, 128), f32),
        ),
        in_specs=[hbm, hbm, vmem, smem, vmem, vmem, vmem, vmem],
        out_specs=(vmem, vmem, vmem, vmem),
        scratch_shapes=[
            pltpu.VMEM((CHUNKS, NZ, NY, width, pool), bf),
            pltpu.VMEM((k, share), f32),
            pltpu.VMEM((CHUNKS, NY, NZ, k, width), bf),
            pltpu.VMEM((ROUNDS, CHUNKS, NY - 1, NZ, k, width), bf),
            pltpu.VMEM((CHUNKS, NZ, k, width), bf),
            pltpu.VMEM((CHUNKS, k, width), f32),
            pltpu.VMEM((ROUNDS, CHUNKS, NZ - 1, k, width), bf),
            pltpu.VMEM((ROUNDS, CHUNKS, NY, NZ, k, width), bf),
            pltpu.VMEM((ROUNDS, k, pool), f32),
            pltpu.VMEM((ROUNDS, NIND, k, pool), f32),
            pltpu.VMEM((8, 128), f32),
            pltpu.VMEM((NY, 8, 128), f32),
            pltpu.VMEM((8, 128), f32),
            pltpu.VMEM((NZ, 8, 128), f32),
            dma((CHUNKS,)),
            dma,
        ] + [dma((ROUNDS, CHUNKS))] * 8 + [dma((ROUNDS,))] * 2 + [dma((2,))] * 2,
        compiler_params=pltpu.CompilerParams(
            collective_id=0, has_side_effects=True, vmem_limit_bytes=48 * 1024 * 1024
        ),
        cost_estimate=pl.CostEstimate(
            flops=2 * 2 * ROUNDS * k * pool * row_dev, bytes_accessed=2 * pool * row_dev, transcendentals=0
        ),
        name="elastic_net_step",
    )(
        dosages.reshape(NZ, NY, CHUNKS, width, pool),
        phenotypes, screen_ids, screen_counts, kkt_ids, coef_prev, coef_slope, penalty.reshape(1, k),
    )
    return (coef, resid, kkt, small[0, :k], small[1, :k])


def solution(mesh):
    placed = (
        P("ind", "var"),
        P(None, "ind"),
        P("var", None),
        P("var"),
        P("var", None),
        P(None, "var"),
        P(None, "var"),
        P(),
    )
    return jax.shard_map(
        body,
        mesh=mesh,
        in_specs=placed,
        out_specs=(P(None, "var"), P(None, ("ind", "var")), P(None, "var"), P(), P()),
        check_vma=False,
    )
```

```python
import functools

import jax
import jax.numpy as jnp
from jax import lax
from jax.experimental import pallas as pl
from jax.experimental.pallas import tpu as pltpu
from jax.sharding import PartitionSpec as P

MESH = pl.DeviceIdType.MESH
SWEEPS = 2
ROUNDS = SWEEPS + 1
NY, NZ = 4, 8
NIND = 8
CHUNKS = 2
GROUPS = 2
NT = (((1,), (1,)), ((), ()))
Z_ORDER = (4, 3, 5, 2, 6, 1, 7)
EXACT = dict(preferred_element_type=jnp.float32, precision=lax.Precision.HIGHEST)
BF, F32 = jnp.bfloat16, jnp.float32

PERIOD, STAGGER, SPACING = 26.0, 8.0, 2.0
OFFSET = {1: 0.0, 2: 5.0, 3: 9.5, 4: 14.0, 5: 18.5, 6: 25.0}


def nominal(step):
    group, r, phase, c = step
    return group * STAGGER + r * PERIOD + OFFSET[phase] + c * (0.6 if phase == 1 else SPACING)


ORDER = [(0, 0, 1, 0), (0, 0, 1, 1), (1, 0, 1, 0), (0, 0, 2, 0), (1, 0, 1, 1), (0, 0, 2, 1), (0, 0, 3, 0), (1, 0, 2, 0), (0, 0, 3, 1), (0, 0, 4, 0), (1, 0, 2, 1), (1, 0, 3, 0), (0, 0, 4, 1), (1, 0, 3, 1), (1, 0, 4, 0), (0, 0, 5, 0), (0, 0, 5, 1), (1, 0, 4, 1), (1, 0, 5, 0), (0, 0, 6, 0), (0, 1, 1, 0), (1, 0, 5, 1), (0, 1, 1, 1), (0, 1, 2, 0), (1, 0, 6, 0), (1, 1, 1, 0), (0, 1, 2, 1), (1, 1, 1, 1), (0, 1, 3, 0), (1, 1, 2, 0), (0, 1, 3, 1), (0, 1, 4, 0), (1, 1, 2, 1), (1, 1, 3, 0), (0, 1, 4, 1), (1, 1, 3, 1), (1, 1, 4, 0), (0, 1, 5, 0), (0, 1, 5, 1), (1, 1, 4, 1), (1, 1, 5, 0), (0, 1, 6, 0), (0, 2, 1, 0), (1, 1, 5, 1), (0, 2, 1, 1), (0, 2, 2, 0), (1, 1, 6, 0), (1, 2, 1, 0), (0, 2, 2, 1), (1, 2, 1, 1), (0, 2, 3, 0), (1, 2, 2, 0), (0, 2, 3, 1), (1, 2, 2, 1), (0, 2, 4, 0), (1, 2, 3, 0), (0, 2, 4, 1), (1, 2, 3, 1), (1, 2, 4, 0), (0, 2, 5, 0), (1, 2, 4, 1), (0, 2, 5, 1), (1, 2, 5, 0), (1, 2, 5, 1), (0, 2, 6, 0), (1, 2, 6, 0)]


def kernel(
    total_rows,
    dosages, phenotypes, screen_ids, screen_counts, kkt_ids, coef_prev, coef_slope, penalty,
    coef_hbm, resid_hbm, kkt_hbm, worst_hbm, objective_hbm,
    coef_out, resid_out, kkt_out, worst_out, objective_out, x, phen, ids_v, counts_s, kkt_v, prev_v, slope_v, pen_v,
    psend, yown, yrecv, zsend, zown, zrecv, gathered, irecv, lrecv, frecv, fzrecv,
    x_sem, in_sem, out_sem, y_s, y_r, z_s, z_r, gz_s, gz_r, gy_s, gy_r, i_s, i_r, f_s, f_r,
):
    ind = lax.axis_index("ind")
    var = lax.axis_index("var")
    z, y = var // NY, lax.rem(var, NY)
    k, cap = prev_v.shape
    width, pool = x.shape[3:]
    share = CHUNKS * width
    kg = k // GROUPS
    batch = kkt_v.shape[1]

    def at_y(step):
        return lax.rem(y + step, NY)

    def at_z(step):
        return lax.rem(z + step, NZ)

    def y_peer(step):
        return (ind, z * NY + at_y(step))

    def z_peer(step):
        return (ind, at_z(step) * NY + y)

    def i_peer(step):
        return (lax.rem(ind + step, NIND), var)

    small = [
        pltpu.make_async_copy(src, dst, in_sem.at[n])
        for n, (src, dst) in enumerate((
            (screen_ids, ids_v), (screen_counts, counts_s), (kkt_ids, kkt_v),
            (coef_prev, prev_v), (coef_slope, slope_v), (penalty, pen_v),
        ))
    ]
    phen_copy = pltpu.make_async_copy(
        phenotypes.at[:, pl.ds(pl.multiple_of(var * share, share), share)], phen, in_sem.at[len(small)]
    )
    x_copies = [pltpu.make_async_copy(dosages.at[:, :, c], x.at[c], x_sem.at[c]) for c in range(CHUNKS)]
    for copy in small + x_copies + [phen_copy]:
        copy.start()

    barrier = pltpu.get_barrier_semaphore()
    for step in range(1, NY):
        pl.semaphore_signal(barrier, inc=1, device_id=y_peer(step), device_id_type=MESH)
    for step in range(1, NZ):
        pl.semaphore_signal(barrier, inc=1, device_id=z_peer(step), device_id_type=MESH)
    for step in range(1, NIND):
        pl.semaphore_signal(barrier, inc=1, device_id=i_peer(step), device_id_type=MESH)

    for copy in small:
        copy.wait()
    live = (lax.broadcasted_iota(jnp.int32, (1, cap), 1) < counts_s[...]).astype(F32)
    spread = (lax.broadcasted_iota(jnp.int32, (pool, cap), 0) == ids_v[:, :cap]).astype(F32)
    pick = (lax.broadcasted_iota(jnp.int32, (pool, batch), 0) == kkt_v[...]).astype(F32)
    diagonal = lax.broadcasted_iota(jnp.int32, (k, k), 0) == lax.broadcasted_iota(jnp.int32, (k, k), 1)
    pen_all = jnp.sum(jnp.where(diagonal, jnp.broadcast_to(pen_v[...], (k, k)), 0.0), axis=1, keepdims=True)
    warm = lax.dot_general(live * (prev_v[...] + 0.5 * slope_v[...]), spread, NT, **EXACT)
    live_col = lax.dot_general(jnp.broadcast_to(live, (kg, cap)), spread, NT, **EXACT)
    members = [slice(g * kg, (g + 1) * kg) for g in range(GROUPS)]
    pens = [pen_all[rows] for rows in members]
    coefs = [warm[rows] for rows in members]
    totals = [None] * GROUPS
    squares = [jnp.zeros((kg, 128), F32)] * GROUPS
    worsts, losses = [None] * GROUPS, [None] * GROUPS

    def remote(src, dst, send, recv, device):
        return pltpu.make_async_remote_copy(
            src_ref=src, dst_ref=dst, send_sem=send, recv_sem=recv, device_id=device, device_id_type=MESH
        )

    written = 0
    puts = []

    def put(src, dst, slot):
        puts.append(pltpu.make_async_copy(src, dst, out_sem.at[slot]))
        puts[-1].start()

    def drain(ref, sem):
        pltpu.make_async_copy(ref, ref, sem).wait()

    def three(g, r, c):
        return gathered.at[r, g, c, pl.ds(0, NY - 1)]

    def seven(g, r, c):
        return gathered.at[r, g, c, 0, pl.ds(0, NZ - 1)]

    for g, r, phase, c in ORDER:
        here = (r, g, c)
        last = r == ROUNDS - 1
        if phase == 1:
            if x_copies[c] is not None:
                x_copies[c].wait()
                x_copies[c] = None
            if r > 0:
                drain(three(g, r, c), y_s.at[r - 1, g, c])
            coef_bf = coefs[g].astype(BF)

            def predict(to):
                for t in range(NZ):
                    psend[g, c, to, t] = lax.dot_general(
                        coef_bf, x[c, t, to], NT, preferred_element_type=F32
                    ).astype(BF)

            @pl.loop(1, NY)
            def _(step):
                to = at_y(step)
                predict(to)
                if (g, r, phase, c) == ORDER[0]:
                    @pl.when(step == 1)
                    def _():
                        pl.semaphore_wait(barrier, NY + NZ + NIND - 3)
                remote(psend.at[g, c, to], yrecv.at[r, g, c, step - 1], y_s.at[here], y_r.at[here], y_peer(step)).start()

            for t in range(NZ):
                yown[g, c, t] = lax.dot_general(coef_bf, x[c, t, y], NT, preferred_element_type=F32)
        elif phase == 2:
            if r > 0:
                drain(seven(g, r, c), z_s.at[r - 1, g, c])
            drain(three(g, r, c), y_r.at[here])
            for step in Z_ORDER + (0,):
                to = at_z(step)
                part = yown[g, c, to]
                for s in range(NY - 1):
                    part = part + yrecv[r, g, c, s, to].astype(F32)
                if step:
                    zsend[g, c, to] = part.astype(BF)
                    remote(zsend.at[g, c, to], zrecv.at[r, g, c, step - 1], z_s.at[here], z_r.at[here], z_peer(step)).start()
                else:
                    zown[g, c] = part
        elif phase == 3:
            drain(seven(g, r, c), z_r.at[here])
            if phen_copy is not None:
                phen_copy.wait()
                phen_copy = None
            pred = zown[g, c]
            for s in range(NZ - 1):
                pred = pred + zrecv[r, g, c, s].astype(F32)
            columns = slice(c * width, (c + 1) * width)
            resid = phen[members[g], columns] - pred
            if last:
                resid_out[members[g], columns] = resid
                written += 1
                if written == GROUPS * CHUNKS:
                    put(resid_out, resid_hbm, 0)
            gathered[r, g, c, y, z] = resid.astype(BF)
            block = gathered.at[r, g, c, y, z]
            for step in Z_ORDER:
                remote(block, block, gz_s.at[here], gz_r.at[here], z_peer(step)).start()
        elif phase in (4, 5):
            if phase == 4:
                drain(seven(g, r, c), gz_r.at[here])
                blocks = gathered.at[r, g, c, y]
                for step in (2, 1, 3):
                    remote(blocks, blocks, gy_s.at[here], gy_r.at[here], y_peer(step)).start()
            else:
                drain(three(g, r, c), gy_r.at[here])

            def contract(of, carry):
                total, square = carry
                for t in range(NZ):
                    block = gathered[r, g, c, of, t]
                    total = total + jnp.dot(block, x[c, t, of], preferred_element_type=F32)
                    if last:
                        wide = block.astype(F32)
                        for lane in range(0, width, 128):
                            square = square + wide[:, lane:lane + 128] * wide[:, lane:lane + 128]
                return total, square

            if phase == 4:
                if c == 0:
                    totals[g] = jnp.zeros((kg, pool), F32)
                carry = contract(y, (totals[g], squares[g]))
            else:
                carry = lax.fori_loop(1, NY, lambda step, carry: contract(at_y(step), carry), (totals[g], squares[g]))
            totals[g], squares[g] = carry
            if phase == 5 and c == CHUNKS - 1:
                if last:
                    loss = jnp.sum(squares[g], axis=1, keepdims=True)
                    kkt_part = jnp.dot(totals[g], pick, **EXACT)
                    lrecv[g, ind] = jnp.concatenate([kkt_part, jnp.broadcast_to(loss, (kg, 128 - batch))], axis=1)
                    slot = lrecv.at[g, ind]
                else:
                    irecv[r, g, ind] = totals[g]
                    slot = irecv.at[r, g, ind]
                for step in (4, 5, 2, 3, 6, 7, 1):
                    remote(slot, slot, i_s.at[r, g], i_r.at[r, g], i_peer(step)).start()
        elif not last:
            drain(irecv.at[r, g, pl.ds(0, NIND - 1)], i_r.at[r, g])
            total = irecv[r, g, 0]
            for s in range(1, NIND):
                total = total + irecv[r, g, s]
            moved = coefs[g] + 0.5 * (total / total_rows)
            shrink = 0.25 * pens[g]
            soft = jnp.maximum(moved - shrink, 0.0) + jnp.minimum(moved + shrink, 0.0)
            coefs[g] = live_col * soft / (1.0 + 0.25 * pens[g])
        else:
            drain(lrecv.at[g, pl.ds(0, NIND - 1)], i_r.at[r, g])
            total = lrecv[g, 0]
            for s in range(1, NIND):
                total = total + lrecv[g, s]
            kkt_grad = total[:, :batch] / total_rows
            kkt_out[members[g]] = kkt_grad
            losses[g] = total[:, batch:batch + 1] / (2.0 * total_rows)
            worsts[g] = jnp.max(jnp.maximum(jnp.abs(kkt_grad) - 0.5 * pens[g], 0.0), axis=1, keepdims=True)

    lanes = lax.broadcasted_iota(jnp.int32, (kg, 128), 1)
    rows = lax.broadcasted_iota(jnp.int32, (kg, 128), 0)

    def as_row(columns):
        return sum(
            jnp.sum(jnp.where(rows + g * kg == lanes, columns[g], 0.0), axis=0, keepdims=True) for g in range(GROUPS)
        )

    pen_part = [
        pens[g] * jnp.sum(0.5 * jnp.abs(coefs[g]) + 0.25 * coefs[g] * coefs[g], axis=1, keepdims=True)
        for g in range(GROUPS)
    ]
    upper = lax.broadcasted_iota(jnp.int32, (8, 128), 0) == 0

    def merge(a, b):
        return jnp.where(upper, jnp.maximum(a, b), a + b)

    frecv[y] = jnp.where(upper, as_row(worsts), as_row(pen_part))
    for step in (2, 1, 3):
        remote(frecv.at[y], frecv.at[y], f_s.at[0], f_r.at[0], y_peer(step)).start()
    for g in range(GROUPS):
        coef_out[members[g]] = jnp.dot(coefs[g], spread, **EXACT)
    put(coef_out, coef_hbm, 1)
    put(kkt_out, kkt_hbm, 2)
    drain(frecv.at[pl.ds(0, NY - 1)], f_r.at[0])
    both = frecv[0]
    for s in range(1, NY):
        both = merge(both, frecv[s])
    fzrecv[z] = both
    for step in Z_ORDER:
        remote(fzrecv.at[z], fzrecv.at[z], f_s.at[1], f_r.at[1], z_peer(step)).start()
    end = ROUNDS - 1
    for g in range(GROUPS):
        for c in range(CHUNKS):
            drain(three(g, end, c), y_s.at[end, g, c])
            drain(seven(g, end, c), z_s.at[end, g, c])
            for r in range(ROUNDS):
                drain(seven(g, r, c), gz_s.at[r, g, c])
                drain(three(g, r, c), gy_s.at[r, g, c])
        for r in range(end):
            drain(irecv.at[r, g, pl.ds(0, NIND - 1)], i_s.at[r, g])
        drain(lrecv.at[g, pl.ds(0, NIND - 1)], i_s.at[end, g])
    drain(frecv.at[pl.ds(0, NY - 1)], f_s.at[0])
    drain(fzrecv.at[pl.ds(0, NZ - 1)], f_r.at[1])
    both = fzrecv[0]
    for s in range(1, NZ):
        both = merge(both, fzrecv[s])
    worst_out[...] = both[:1, :k]
    objective_out[...] = (both[1:2] + as_row(losses))[:, :k]
    put(worst_out, worst_hbm, 3)
    put(objective_out, objective_hbm, 4)
    drain(fzrecv.at[pl.ds(0, NZ - 1)], f_s.at[1])
    for copy in puts:
        copy.wait()


def hand_over(*refs):
    n = len(refs) // 2
    for source, target in zip(refs[:n], refs[n:]):
        target[...] = source[...]


def body(dosages, phenotypes, screen_ids, screen_counts, kkt_ids, coef_prev, coef_slope, penalty):
    row_dev, pool = dosages.shape
    k, cap = coef_prev.shape
    batch = kkt_ids.shape[1]
    share = row_dev // lax.axis_size("var")
    width = share // CHUNKS
    kg = k // GROUPS
    hbm = pl.BlockSpec(memory_space=pl.ANY)
    dma = pltpu.SemaphoreType.DMA
    each = (ROUNDS, GROUPS, CHUNKS)
    shapes = [(k, cap), (k, share), (k, batch), (1, k), (1, k)]
    results = pl.pallas_call(
        functools.partial(kernel, row_dev * lax.axis_size("ind")),
        out_shape=[jax.ShapeDtypeStruct(shape, F32) for shape in shapes],
        in_specs=[hbm] * 8,
        out_specs=[hbm] * 5,
        scratch_shapes=[
            pltpu.VMEM((k, cap), F32),
            pltpu.VMEM((k, share), F32),
            pltpu.VMEM((k, batch), F32),
            pltpu.VMEM((1, k), F32),
            pltpu.VMEM((1, k), F32),
            pltpu.VMEM((CHUNKS, NZ, NY, width, pool), BF),
            pltpu.VMEM((k, share), F32),
            pltpu.VMEM(screen_ids.shape, jnp.int32),
            pltpu.VMEM((1, 1), jnp.int32),
            pltpu.VMEM(kkt_ids.shape, jnp.int32),
            pltpu.VMEM((k, cap), F32),
            pltpu.VMEM((k, cap), F32),
            pltpu.VMEM((1, k), F32),
            pltpu.VMEM((GROUPS, CHUNKS, NY, NZ, kg, width), BF),
            pltpu.VMEM((GROUPS, CHUNKS, NZ, kg, width), F32),
            pltpu.VMEM(each + (NY - 1, NZ, kg, width), BF),
            pltpu.VMEM((GROUPS, CHUNKS, NZ, kg, width), BF),
            pltpu.VMEM((GROUPS, CHUNKS, kg, width), F32),
            pltpu.VMEM(each + (NZ - 1, kg, width), BF),
            pltpu.VMEM(each + (NY, NZ, kg, width), BF),
            pltpu.VMEM((SWEEPS, GROUPS, NIND, kg, pool), F32),
            pltpu.VMEM((GROUPS, NIND, kg, 128), F32),
            pltpu.VMEM((NY, 8, 128), F32),
            pltpu.VMEM((NZ, 8, 128), F32),
            dma((CHUNKS,)),
            dma((7,)),
            dma((5,)),
        ] + [dma(each)] * 8 + [dma((ROUNDS, GROUPS))] * 2 + [dma((2,))] * 2,
        compiler_params=pltpu.CompilerParams(
            collective_id=0, has_side_effects=True, vmem_limit_bytes=56 * 1024 * 1024
        ),
        cost_estimate=pl.CostEstimate(
            flops=2 * 2 * ROUNDS * k * pool * row_dev, bytes_accessed=2 * pool * row_dev, transcendentals=0
        ),
        name="elastic_net_step",
    )(
        dosages.reshape(NZ, NY, CHUNKS, width, pool),
        phenotypes, screen_ids, screen_counts.reshape(1, 1), kkt_ids, coef_prev, coef_slope, penalty.reshape(1, k),
    )
    coef, resid, kkt, worst, objective = pl.pallas_call(
        hand_over,
        out_shape=[jax.ShapeDtypeStruct(shape, F32) for shape in shapes],

        name="hand_over",
    )(*results)
    return (coef, resid, kkt, worst.reshape(k), objective.reshape(k))


def solution(mesh):
    placed = (
        P("ind", "var"),
        P(None, "ind"),
        P("var", None),
        P("var"),
        P("var", None),
        P(None, "var"),
        P(None, "var"),
        P(),
    )
    return jax.shard_map(
        body,
        mesh=mesh,
        in_specs=placed,
        out_specs=(P(None, "var"), P(None, ("ind", "var")), P(None, "var"), P(), P()),
        check_vma=False,
    )
```

```python
import functools

import jax
import jax.numpy as jnp
from jax import lax
from jax.experimental import pallas as pl
from jax.experimental.pallas import tpu as pltpu
from jax.sharding import PartitionSpec as P

MESH = pl.DeviceIdType.MESH
SWEEPS = 2
ROUNDS = SWEEPS + 1
NY, NZ = 4, 8
NIND = 8
CHUNKS = 2
GROUPS = 2
NT = (((1,), (1,)), ((), ()))
Z_ORDER = (4, 3, 5, 2, 6, 1, 7)
EXACT = dict(preferred_element_type=jnp.float32, precision=lax.Precision.HIGHEST)
BF, F32 = jnp.bfloat16, jnp.float32

PERIOD, STAGGER, SPACING = 26.0, 8.0, 2.0
OFFSET = {1: 0.0, 2: 5.0, 3: 9.5, 4: 14.0, 5: 18.5, 6: 25.0}


def nominal(step):
    group, r, phase, c = step
    return group * STAGGER + r * PERIOD + OFFSET[phase] + c * (0.6 if phase == 1 else SPACING)


ORDER = [(0, 0, 1, 0), (0, 0, 1, 1), (1, 0, 1, 0), (0, 0, 2, 0), (1, 0, 1, 1), (0, 0, 2, 1), (0, 0, 3, 0), (1, 0, 2, 0), (0, 0, 3, 1), (0, 0, 4, 0), (1, 0, 2, 1), (1, 0, 3, 0), (0, 0, 4, 1), (1, 0, 3, 1), (1, 0, 4, 0), (0, 0, 5, 0), (0, 0, 5, 1), (1, 0, 4, 1), (1, 0, 5, 0), (0, 0, 6, 0), (0, 1, 1, 0), (1, 0, 5, 1), (0, 1, 1, 1), (0, 1, 2, 0), (1, 0, 6, 0), (1, 1, 1, 0), (0, 1, 2, 1), (1, 1, 1, 1), (0, 1, 3, 0), (1, 1, 2, 0), (0, 1, 3, 1), (0, 1, 4, 0), (1, 1, 2, 1), (1, 1, 3, 0), (0, 1, 4, 1), (1, 1, 3, 1), (1, 1, 4, 0), (0, 1, 5, 0), (0, 1, 5, 1), (1, 1, 4, 1), (1, 1, 5, 0), (0, 1, 6, 0), (0, 2, 1, 0), (1, 1, 5, 1), (0, 2, 1, 1), (0, 2, 2, 0), (1, 1, 6, 0), (1, 2, 1, 0), (0, 2, 2, 1), (1, 2, 1, 1), (0, 2, 3, 0), (1, 2, 2, 0), (0, 2, 3, 1), (1, 2, 2, 1), (0, 2, 4, 0), (1, 2, 3, 0), (0, 2, 4, 1), (1, 2, 3, 1), (1, 2, 4, 0), (0, 2, 5, 0), (1, 2, 4, 1), (0, 2, 5, 1), (1, 2, 5, 0), (1, 2, 5, 1), (0, 2, 6, 0), (1, 2, 6, 0)]


def kernel(
    total_rows,
    dosages, phenotypes, screen_ids, screen_counts, kkt_ids, coef_prev, coef_slope, penalty,
    coef_hbm, resid_hbm, kkt_hbm, worst_hbm, objective_hbm,
    coef_out, resid_out, kkt_out, worst_out, objective_out, x, phen, ids_v, counts_s, kkt_v, prev_v, slope_v, pen_v,
    psend, yown, yrecv, zsend, zown, zrecv, gathered, irecv, lrecv, frecv, fzrecv,
    x_sem, in_sem, out_sem, y_s, y_r, z_s, z_r, gz_s, gz_r, gy_s, gy_r, i_s, i_r, f_s, f_r,
):
    ind = lax.axis_index("ind")
    var = lax.axis_index("var")
    z, y = var // NY, lax.rem(var, NY)
    k, cap = prev_v.shape
    width, pool = x.shape[3:]
    share = CHUNKS * width
    kg = k // GROUPS
    batch = kkt_v.shape[1]

    def at_y(step):
        return lax.rem(y + step, NY)

    def at_z(step):
        return lax.rem(z + step, NZ)

    def y_peer(step):
        return (ind, z * NY + at_y(step))

    def z_peer(step):
        return (ind, at_z(step) * NY + y)

    def i_peer(step):
        return (lax.rem(ind + step, NIND), var)

    small = [
        pltpu.make_async_copy(src, dst, in_sem.at[n])
        for n, (src, dst) in enumerate((
            (screen_ids, ids_v), (screen_counts, counts_s), (kkt_ids, kkt_v),
            (coef_prev, prev_v), (coef_slope, slope_v), (penalty, pen_v),
        ))
    ]
    phen_copy = pltpu.make_async_copy(
        phenotypes.at[:, pl.ds(pl.multiple_of(var * share, share), share)], phen, in_sem.at[len(small)]
    )
    x_copies = [pltpu.make_async_copy(dosages.at[:, :, c], x.at[c], x_sem.at[c]) for c in range(CHUNKS)]
    for copy in small + x_copies + [phen_copy]:
        copy.start()

    barrier = pltpu.get_barrier_semaphore()
    for step in range(1, NY):
        pl.semaphore_signal(barrier, inc=1, device_id=y_peer(step), device_id_type=MESH)
    for step in range(1, NZ):
        pl.semaphore_signal(barrier, inc=1, device_id=z_peer(step), device_id_type=MESH)
    for step in range(1, NIND):
        pl.semaphore_signal(barrier, inc=1, device_id=i_peer(step), device_id_type=MESH)

    for copy in small:
        copy.wait()
    live = (lax.broadcasted_iota(jnp.int32, (1, cap), 1) < counts_s[...]).astype(F32)
    spread = (lax.broadcasted_iota(jnp.int32, (pool, cap), 0) == ids_v[:, :cap]).astype(F32)
    pick = (lax.broadcasted_iota(jnp.int32, (pool, batch), 0) == kkt_v[...]).astype(F32)
    diagonal = lax.broadcasted_iota(jnp.int32, (k, k), 0) == lax.broadcasted_iota(jnp.int32, (k, k), 1)
    pen_all = jnp.sum(jnp.where(diagonal, jnp.broadcast_to(pen_v[...], (k, k)), 0.0), axis=1, keepdims=True)
    warm = lax.dot_general(live * (prev_v[...] + 0.5 * slope_v[...]), spread, NT, **EXACT)
    live_col = lax.dot_general(jnp.broadcast_to(live, (kg, cap)), spread, NT, **EXACT)
    members = [slice(g * kg, (g + 1) * kg) for g in range(GROUPS)]
    pens = [pen_all[rows] for rows in members]
    coefs = [warm[rows] for rows in members]
    totals = [None] * GROUPS
    squares = [jnp.zeros((kg, 128), F32)] * GROUPS
    worsts, losses = [None] * GROUPS, [None] * GROUPS

    def remote(src, dst, send, recv, device):
        return pltpu.make_async_remote_copy(
            src_ref=src, dst_ref=dst, send_sem=send, recv_sem=recv, device_id=device, device_id_type=MESH
        )

    written = 0
    puts = []

    def put(src, dst, slot):
        puts.append(pltpu.make_async_copy(src, dst, out_sem.at[slot]))
        puts[-1].start()

    def drain(ref, sem):
        pltpu.make_async_copy(ref, ref, sem).wait()

    def three(g, r, c):
        return gathered.at[r, g, c, pl.ds(0, NY - 1)]

    def seven(g, r, c):
        return gathered.at[r, g, c, 0, pl.ds(0, NZ - 1)]

    for g, r, phase, c in ORDER:
        here = (r, g, c)
        last = r == ROUNDS - 1
        if phase == 1:
            if x_copies[c] is not None:
                x_copies[c].wait()
                x_copies[c] = None
            if r > 0:
                drain(three(g, r, c), y_s.at[r - 1, g, c])
            coef_bf = coefs[g].astype(BF)

            def predict(to):
                for t in range(NZ):
                    psend[g, c, to, t] = lax.dot_general(
                        coef_bf, x[c, t, to], NT, preferred_element_type=F32
                    ).astype(BF)

            for step in (1, 2, 3):
                to = at_y(step)
                predict(to)
                if (g, r, phase, c, step) == ORDER[0] + (1,):
                    pl.semaphore_wait(barrier, NY + NZ + NIND - 3)
                remote(psend.at[g, c, to], yrecv.at[r, g, c, step - 1], y_s.at[here], y_r.at[here], y_peer(step)).start()

            for t in range(NZ):
                yown[g, c, t] = lax.dot_general(coef_bf, x[c, t, y], NT, preferred_element_type=F32)
        elif phase == 2:
            if r > 0:
                drain(seven(g, r, c), z_s.at[r - 1, g, c])
            drain(three(g, r, c), y_r.at[here])
            for step in Z_ORDER + (0,):
                to = at_z(step)
                part = yown[g, c, to]
                for s in range(NY - 1):
                    part = part + yrecv[r, g, c, s, to].astype(F32)
                if step:
                    zsend[g, c, to] = part.astype(BF)
                    remote(zsend.at[g, c, to], zrecv.at[r, g, c, step - 1], z_s.at[here], z_r.at[here], z_peer(step)).start()
                else:
                    zown[g, c] = part
        elif phase == 3:
            drain(seven(g, r, c), z_r.at[here])
            if phen_copy is not None:
                phen_copy.wait()
                phen_copy = None
            pred = zown[g, c]
            for s in range(NZ - 1):
                pred = pred + zrecv[r, g, c, s].astype(F32)
            columns = slice(c * width, (c + 1) * width)
            resid = phen[members[g], columns] - pred
            if last:
                resid_out[members[g], columns] = resid
                written += 1
                if written == GROUPS * CHUNKS:
                    put(resid_out, resid_hbm, 0)
            gathered[r, g, c, y, z] = resid.astype(BF)
            block = gathered.at[r, g, c, y, z]
            for step in Z_ORDER:
                remote(block, block, gz_s.at[here], gz_r.at[here], z_peer(step)).start()
        elif phase in (4, 5):
            if phase == 4:
                drain(seven(g, r, c), gz_r.at[here])
                blocks = gathered.at[r, g, c, y]
                for step in (2, 1, 3):
                    remote(blocks, blocks, gy_s.at[here], gy_r.at[here], y_peer(step)).start()
            else:
                drain(three(g, r, c), gy_r.at[here])

            def contract(of, carry):
                total, square = carry
                for t in range(NZ):
                    block = gathered[r, g, c, of, t]
                    total = total + jnp.dot(block, x[c, t, of], preferred_element_type=F32)
                    if last:
                        wide = block.astype(F32)
                        for lane in range(0, width, 128):
                            square = square + wide[:, lane:lane + 128] * wide[:, lane:lane + 128]
                return total, square

            if phase == 4:
                if c == 0:
                    totals[g] = jnp.zeros((kg, pool), F32)
                carry = contract(y, (totals[g], squares[g]))
            else:
                carry = lax.fori_loop(1, NY, lambda step, carry: contract(at_y(step), carry), (totals[g], squares[g]))
            totals[g], squares[g] = carry
            if phase == 5 and c == CHUNKS - 1:
                if last:
                    loss = jnp.sum(squares[g], axis=1, keepdims=True)
                    kkt_part = jnp.dot(totals[g], pick, **EXACT)
                    lrecv[g, ind] = jnp.concatenate([kkt_part, jnp.broadcast_to(loss, (kg, 128 - batch))], axis=1)
                    slot = lrecv.at[g, ind]
                else:
                    irecv[r, g, ind] = totals[g]
                    slot = irecv.at[r, g, ind]
                for step in (4, 5, 2, 3, 6, 7, 1):
                    remote(slot, slot, i_s.at[r, g], i_r.at[r, g], i_peer(step)).start()
        elif not last:
            drain(irecv.at[r, g, pl.ds(0, NIND - 1)], i_r.at[r, g])
            total = irecv[r, g, 0]
            for s in range(1, NIND):
                total = total + irecv[r, g, s]
            moved = coefs[g] + 0.5 * (total / total_rows)
            shrink = 0.25 * pens[g]
            soft = jnp.maximum(moved - shrink, 0.0) + jnp.minimum(moved + shrink, 0.0)
            coefs[g] = live_col * soft / (1.0 + 0.25 * pens[g])
        else:
            drain(lrecv.at[g, pl.ds(0, NIND - 1)], i_r.at[r, g])
            total = lrecv[g, 0]
            for s in range(1, NIND):
                total = total + lrecv[g, s]
            kkt_grad = total[:, :batch] / total_rows
            kkt_out[members[g]] = kkt_grad
            losses[g] = total[:, batch:batch + 1] / (2.0 * total_rows)
            worsts[g] = jnp.max(jnp.maximum(jnp.abs(kkt_grad) - 0.5 * pens[g], 0.0), axis=1, keepdims=True)

    lanes = lax.broadcasted_iota(jnp.int32, (kg, 128), 1)
    rows = lax.broadcasted_iota(jnp.int32, (kg, 128), 0)

    def as_row(columns):
        return sum(
            jnp.sum(jnp.where(rows + g * kg == lanes, columns[g], 0.0), axis=0, keepdims=True) for g in range(GROUPS)
        )

    pen_part = [
        pens[g] * jnp.sum(0.5 * jnp.abs(coefs[g]) + 0.25 * coefs[g] * coefs[g], axis=1, keepdims=True)
        for g in range(GROUPS)
    ]
    upper = lax.broadcasted_iota(jnp.int32, (8, 128), 0) == 0

    def merge(a, b):
        return jnp.where(upper, jnp.maximum(a, b), a + b)

    frecv[y] = jnp.where(upper, as_row(worsts), as_row(pen_part))
    for step in (2, 1, 3):
        remote(frecv.at[y], frecv.at[y], f_s.at[0], f_r.at[0], y_peer(step)).start()
    for g in range(GROUPS):
        coef_out[members[g]] = jnp.dot(coefs[g], spread, **EXACT)
    put(coef_out, coef_hbm, 1)
    put(kkt_out, kkt_hbm, 2)
    drain(frecv.at[pl.ds(0, NY - 1)], f_r.at[0])
    both = frecv[0]
    for s in range(1, NY):
        both = merge(both, frecv[s])
    fzrecv[z] = both
    for step in Z_ORDER:
        remote(fzrecv.at[z], fzrecv.at[z], f_s.at[1], f_r.at[1], z_peer(step)).start()
    end = ROUNDS - 1
    for g in range(GROUPS):
        for c in range(CHUNKS):
            drain(three(g, end, c), y_s.at[end, g, c])
            drain(seven(g, end, c), z_s.at[end, g, c])
            for r in range(ROUNDS):
                drain(seven(g, r, c), gz_s.at[r, g, c])
                drain(three(g, r, c), gy_s.at[r, g, c])
        for r in range(end):
            drain(irecv.at[r, g, pl.ds(0, NIND - 1)], i_s.at[r, g])
        drain(lrecv.at[g, pl.ds(0, NIND - 1)], i_s.at[end, g])
    drain(frecv.at[pl.ds(0, NY - 1)], f_s.at[0])
    drain(fzrecv.at[pl.ds(0, NZ - 1)], f_r.at[1])
    both = fzrecv[0]
    for s in range(1, NZ):
        both = merge(both, fzrecv[s])
    worst_out[...] = both[:1, :k]
    objective_out[...] = (both[1:2] + as_row(losses))[:, :k]
    put(worst_out, worst_hbm, 3)
    put(objective_out, objective_hbm, 4)
    drain(fzrecv.at[pl.ds(0, NZ - 1)], f_s.at[1])
    for copy in puts:
        copy.wait()


def hand_over(*refs):
    n = len(refs) // 2
    for source, target in zip(refs[:n], refs[n:]):
        target[...] = source[...]


def body(dosages, phenotypes, screen_ids, screen_counts, kkt_ids, coef_prev, coef_slope, penalty):
    row_dev, pool = dosages.shape
    k, cap = coef_prev.shape
    batch = kkt_ids.shape[1]
    share = row_dev // lax.axis_size("var")
    width = share // CHUNKS
    kg = k // GROUPS
    hbm = pl.BlockSpec(memory_space=pl.ANY)
    dma = pltpu.SemaphoreType.DMA
    each = (ROUNDS, GROUPS, CHUNKS)
    shapes = [(k, cap), (k, share), (k, batch), (1, k), (1, k)]
    results = pl.pallas_call(
        functools.partial(kernel, row_dev * lax.axis_size("ind")),
        out_shape=[jax.ShapeDtypeStruct(shape, F32) for shape in shapes],
        in_specs=[hbm] * 8,
        out_specs=[hbm] * 5,
        scratch_shapes=[
            pltpu.VMEM((k, cap), F32),
            pltpu.VMEM((k, share), F32),
            pltpu.VMEM((k, batch), F32),
            pltpu.VMEM((1, k), F32),
            pltpu.VMEM((1, k), F32),
            pltpu.VMEM((CHUNKS, NZ, NY, width, pool), BF),
            pltpu.VMEM((k, share), F32),
            pltpu.VMEM(screen_ids.shape, jnp.int32),
            pltpu.VMEM((1, 1), jnp.int32),
            pltpu.VMEM(kkt_ids.shape, jnp.int32),
            pltpu.VMEM((k, cap), F32),
            pltpu.VMEM((k, cap), F32),
            pltpu.VMEM((1, k), F32),
            pltpu.VMEM((GROUPS, CHUNKS, NY, NZ, kg, width), BF),
            pltpu.VMEM((GROUPS, CHUNKS, NZ, kg, width), F32),
            pltpu.VMEM(each + (NY - 1, NZ, kg, width), BF),
            pltpu.VMEM((GROUPS, CHUNKS, NZ, kg, width), BF),
            pltpu.VMEM((GROUPS, CHUNKS, kg, width), F32),
            pltpu.VMEM(each + (NZ - 1, kg, width), BF),
            pltpu.VMEM(each + (NY, NZ, kg, width), BF),
            pltpu.VMEM((SWEEPS, GROUPS, NIND, kg, pool), F32),
            pltpu.VMEM((GROUPS, NIND, kg, 128), F32),
            pltpu.VMEM((NY, 8, 128), F32),
            pltpu.VMEM((NZ, 8, 128), F32),
            dma((CHUNKS,)),
            dma((7,)),
            dma((5,)),
        ] + [dma(each)] * 8 + [dma((ROUNDS, GROUPS))] * 2 + [dma((2,))] * 2,
        compiler_params=pltpu.CompilerParams(
            collective_id=0, has_side_effects=True, vmem_limit_bytes=56 * 1024 * 1024
        ),
        cost_estimate=pl.CostEstimate(
            flops=2 * 2 * ROUNDS * k * pool * row_dev, bytes_accessed=2 * pool * row_dev, transcendentals=0
        ),
        name="elastic_net_step",
    )(
        dosages.reshape(NZ, NY, CHUNKS, width, pool),
        phenotypes, screen_ids, screen_counts.reshape(1, 1), kkt_ids, coef_prev, coef_slope, penalty.reshape(1, k),
    )
    coef, resid, kkt, worst, objective = pl.pallas_call(
        hand_over,
        out_shape=[jax.ShapeDtypeStruct(shape, F32) for shape in shapes],

        name="hand_over",
    )(*results)
    return (coef, resid, kkt, worst.reshape(k), objective.reshape(k))


def solution(mesh):
    placed = (
        P("ind", "var"),
        P(None, "ind"),
        P("var", None),
        P("var"),
        P("var", None),
        P(None, "var"),
        P(None, "var"),
        P(),
    )
    return jax.shard_map(
        body,
        mesh=mesh,
        in_specs=placed,
        out_specs=(P(None, "var"), P(None, ("ind", "var")), P(None, "var"), P(), P()),
        check_vma=False,
    )
```
